32 devices in a mesh: parts: 1, dp: 32 (over z, y, x, core).
Axes of the slice: x: 2, y: 2, z: 4, core: 2. Of those that a mesh axis runs over, the one named last changes fastest.
Arguments:
- activations: bfloat16 [5120, 4, 3072], P(('parts', 'dp')), may hold values from -6 to 6
- out_grads: bfloat16 [5120, 4, 6144], P(('parts', 'dp')), may hold values from -6 to 6
- input_proj: bfloat16 [3072, 32], replicated, may hold values from -0.109375 to 0.109375
- output_proj: bfloat16 [6144, 32], replicated, may hold values from -0.078125 to 0.078125
- time_weight: float32 [8], replicated, may hold values from 0.2 to 5
- time_index: int32 [5120], P(('parts', 'dp')), may hold values from 0 to 7
- pair_ids: int32 [5120], P(('parts', 'dp')), may hold values from 0 to 5119, each once
- query_ids: int32 [128], P('parts'), may hold values from 0 to 5119
Outputs:
- scores: float32 [5120, 128], P(('parts', 'dp'))
- preconditioned: float32 [1024, 128], P('dp', 'parts')
The draws below stay inside these ranges and needn't reach their ends.
Inputs may be any that keep to these rules, and one draw needn't show every extreme that they name: `pair_ids`: every pair id appears exactly once.
All inputs are finite; a program needn't handle non-finite values.
Results may differ from the reference program's by a relative error of at most 0.0003.
Values sent between devices are 32-bit elements; how exact they have to be, the bound alone decides.
A program may use at most 64 MiB of HBM per device.

```python
import math
import jax
import jax.numpy as jnp
from jax import lax

D_IN = 3072
D_OUT = 6144
LOW = 32
TOK = 4
NQ = 128
TSTEPS = 8
ITERS = 4
FEAT = 1024
PAIRS = 5120


def set_ends(values, stream_key, low, top_value):
    place = [jax.random.randint(jax.random.fold_in(stream_key, axis), (), 0, length) for axis, length in enumerate(values.shape)]
    longest = values.shape.index(max(values.shape))
    next_to = place[:longest] + [(place[longest] + 1) % values.shape[longest]] + place[longest + 1:]
    return values.at[tuple(place)].set(low).at[tuple(next_to)].set(top_value)


def block_levels(own_key, dims, cuts, low, high):
    factor_of, own = 1.0, jax.random.fold_in(own_key, 6)
    for dim, shards_of in cuts:
        heights = jnp.exp(jax.random.uniform(jax.random.fold_in(own, dim), (shards_of,), jnp.float32, low / len(cuts), high / len(cuts)))
        factor_of = factor_of * jnp.repeat(heights, dims[dim] // shards_of).reshape([-1 if axis == dim else 1 for axis in range(len(dims))])
    return factor_of


def gaussian(stream_key, shape, deviation, limit, split=(), held_as=jnp.bfloat16):
    array = deviation * jax.random.normal(stream_key, shape, jnp.float32)
    if split:
        array = array * block_levels(stream_key, shape, split, -0.22, 0.18)
    return jnp.clip(array, -limit, limit).astype(held_as)


def setup_inputs(seed: int = 0, part: int = 0) -> dict:
    seeds = jax.random.split(jax.random.key(seed), 9)
    part_keys = jax.random.split(jax.random.fold_in(seeds[8], part), 9)
    activations = gaussian(part_keys[0], (PAIRS, TOK, D_IN), 1.0, 6.0, ((0, 32),))
    out_grads = gaussian(part_keys[1], (PAIRS, TOK, D_OUT), 1.0, 6.0, ((0, 32),))
    input_proj = gaussian(seeds[2], (D_IN, LOW), D_IN ** -0.5, 0.109375)
    output_proj = gaussian(seeds[3], (D_OUT, LOW), D_OUT ** -0.5, 0.078125)
    time_weight = jnp.clip(jnp.exp(jax.random.uniform(seeds[4], (TSTEPS,), jnp.float32, math.log(0.2), math.log(5.0))), 0.2, 5.0)
    time_index = set_ends(jax.random.randint(part_keys[5], (PAIRS,), 0, TSTEPS), jax.random.fold_in(part_keys[5], 1), 0, TSTEPS - 1).astype(jnp.int32)
    pair_ids = jax.random.permutation(part_keys[6], PAIRS).astype(jnp.int32)
    query_ids = set_ends(jax.random.randint(part_keys[7], (NQ,), 0, PAIRS), jax.random.fold_in(part_keys[7], 1), 0, PAIRS - 1).astype(jnp.int32)
    return {"activations": activations, "out_grads": out_grads, "input_proj": input_proj, "output_proj": output_proj, "time_weight": time_weight, "time_index": time_index, "pair_ids": pair_ids, "query_ids": query_ids}


damping = 0.5


def reference(activations, out_grads, input_proj, output_proj, time_weight, time_index, pair_ids, query_ids):
    highest = lax.Precision.HIGHEST
    act_low = jnp.dot(activations.reshape(-1, D_IN), input_proj, preferred_element_type=jnp.float32).reshape(PAIRS, TOK, LOW)
    grad_low = jnp.dot(out_grads.reshape(-1, D_OUT), output_proj, preferred_element_type=jnp.float32).reshape(PAIRS, TOK, LOW)
    features = jnp.einsum("ptj,pti->pji", grad_low, act_low, precision=highest).reshape(PAIRS, FEAT)
    loss_weight = time_weight[time_index]
    fisher = jnp.dot((features * (loss_weight / PAIRS)[:, None]).T, features, precision=highest)
    fisher = fisher + damping * jnp.eye(FEAT, dtype=jnp.float32)
    inverse = jnp.zeros((PAIRS,), jnp.int32).at[pair_ids].set(jnp.arange(PAIRS, dtype=jnp.int32))
    query = features[inverse[query_ids]].T
    solution = jnp.zeros_like(query)
    residual = query
    direction = query
    norm_now = jnp.sum(residual * residual, axis=0)
    for sweep_index in range(ITERS):
        image = jnp.dot(fisher, direction, precision=highest)
        step_size = norm_now / jnp.sum(direction * image, axis=0)
        solution = solution + step_size * direction
        residual = residual - step_size * image
        if sweep_index + 1 < ITERS:
            norm_next = jnp.sum(residual * residual, axis=0)
            direction = residual + (norm_next / norm_now) * direction
            norm_now = norm_next
    scores = jnp.dot(features, solution, precision=highest) * loss_weight[:, None] * (FEAT ** -0.5)
    return scores, solution
```

```python
import functools

import jax
import jax.numpy as jnp
from jax import lax
from jax.experimental import pallas as pl
from jax.experimental.pallas import tpu as pltpu
from jax.sharding import PartitionSpec as P

ITERS = 4
DAMPING = 0.5
GROUP = 8
BANDS = GROUP // 2 + 1
F32 = jnp.float32
BF16 = jnp.bfloat16


def split(value):
    high = value.astype(BF16)
    return high, (value - high.astype(F32)).astype(BF16)


def dot_nt(a, b):
    return lax.dot_general(a, b, (((1,), (1,)), ((), ())), preferred_element_type=F32)


def flip(index, bits):
    out = index
    for bit in (1, 2, 4):
        if bits & bit:
            out = out + bit - 2 * bit * ((index // bit) % 2)
    return out


def kernel(
    count, tokens, low, pairs, msg_ref, query_ref, weight_ref, scores_ref, own_ref,
    fac, fac_t, own_t, local_t, local, feats, part, landed, fis, qpart, qlanded, qf, query,
    f_high, f_low, x_ref,
    fac_send, fac_recv, rs_send, rs_recv, qz_send, qz_recv, ag_send, ag_recv,
    fis_send, fis_recv, qf_send, qf_recv,
):
    me = lax.axis_index("dp")
    spot = me % GROUP
    base = me - spot
    level = me // GROUP
    levels = count // GROUP
    feat = low * low
    block = feat // GROUP
    piece = block // levels
    per_block = block // low
    near = (2, 4, 6)

    def send(src, dst, send_sem, recv_sem, peer):
        copy = pltpu.make_async_remote_copy(
            src_ref=src, dst_ref=dst, send_sem=send_sem, recv_sem=recv_sem,
            device_id={"dp": peer}, device_id_type=pl.DeviceIdType.MESH,
        )
        copy.start()
        return copy

    def level_peer(step):
        return ((level + step) % levels) * GROUP + spot

    class Gather:
        def __init__(self, buffer, send_sem, recv_sem, source=None):
            self.buffer, self.send_sem, self.recv_sem = buffer, send_sem, recv_sem
            src = buffer.at[spot] if source is None else source
            self.copies = {}
            for bits in near + (1,):
                self.copies[bits] = send(
                    src, buffer.at[spot], send_sem.at[bits - 1], recv_sem.at[bits - 1],
                    base + flip(spot, bits),
                )

        def relay(self):
            for bits in near:
                self.copies[bits].wait_recv()
                there = self.buffer.at[flip(spot, bits)]
                self.copies[bits + 1] = send(
                    there, there, self.send_sem.at[bits], self.recv_sem.at[bits],
                    base + flip(spot, 1),
                )

        def finish(self):
            for bits in (1, 3, 5, 7):
                self.copies[bits].wait_recv()
            for bits in range(1, GROUP):
                self.copies[bits].wait_send()

    barrier = pltpu.get_barrier_semaphore()
    peers = [base + flip(spot, bits) for bits in (1,) + near]
    peers += [level_peer(step) for step in range(1, levels)]
    for peer in peers:
        pl.semaphore_signal(
            barrier, inc=1, device_id={"dp": peer}, device_id_type=pl.DeviceIdType.MESH
        )
    pl.semaphore_wait(barrier, len(peers))

    gather = Gather(fac, fac_send, fac_recv, msg_ref)
    fac[spot] = msg_ref[...]

    own_t[...] = msg_ref[0:pairs, :].T

    def expand(read_row, act, out, start):
        total = None
        for t in range(tokens):
            term = read_row(t) * act(t)
            total = term if total is None else total + term
        out[pl.ds(start, low), :] = total

    half = tokens * low

    @pl.loop(0, low)
    def _(j):
        expand(
            lambda t: own_t[pl.ds(half + t * low + j, 1), :],
            lambda t: own_t[t * low:(t + 1) * low, :],
            local_t, pl.multiple_of(j * low, low),
        )

    local[...] = local_t[...].T

    gather.relay()
    gather.finish()

    fac_t[...] = jnp.concatenate([fac[s, 0:pairs, :] for s in range(GROUP)], axis=0).T
    extras = jnp.concatenate([fac[s, pairs:pairs + 8, 0:pairs] for s in range(GROUP)], axis=1)
    weights = extras[0:1, :]
    ids = extras[1:2, :]

    chosen = jnp.where(query_ref[...] == ids, 1.0, 0.0).astype(BF16)
    share = 2 * half // GROUP
    rows = fac_t[pl.ds(pl.multiple_of(spot * share, share), share), :]
    high, rest = rows.astype(BF16), rows
    rest = rest - high.astype(F32)
    mid, last = split(rest)
    qpart[...] = (dot_nt(last, chosen) + dot_nt(mid, chosen)) + dot_nt(high, chosen)
    q_copies = [
        send(qpart, qlanded.at[k - 1], qz_send.at[k - 1], qz_recv.at[k - 1], level_peer(k))
        for k in range(1, levels)
    ]

    for b in range(BANDS):
        first = ((spot + b) % GROUP) * per_block

        @pl.loop(0, per_block)
        def _(jj):
            expand(
                lambda t: fac_t[pl.ds(half + t * low + first + jj, 1), :],
                lambda t: fac_t[t * low:(t + 1) * low, :],
                feats, pl.multiple_of(b * block + jj * low, low),
            )

    a_high, a_low = split(feats[0:block, :] * weights)
    for b in range(BANDS):
        b_high, b_low = split(feats[b * block:(b + 1) * block, :])
        part[:, b * block:(b + 1) * block] = (
            dot_nt(a_low, b_high) + dot_nt(a_high, b_low)
        ) + dot_nt(a_high, b_high)

    def rows_of(lv):
        return pl.ds(pl.multiple_of(lv * piece, piece), piece)

    rs_copies = [
        send(
            part.at[rows_of((level + k) % levels), :], landed.at[k - 1],
            rs_send.at[k - 1], rs_recv.at[k - 1], level_peer(k),
        )
        for k in range(1, levels)
    ]
    q_total = qpart[...]
    for k in range(1, levels):
        q_copies[k - 1].wait_recv()
        q_total = q_total + qlanded[k - 1]
    qf[spot] = q_total
    q_gather = Gather(qf, qf_send, qf_recv)

    total = part[rows_of(level), :]
    for k in range(1, levels):
        rs_copies[k - 1].wait_recv()
        total = total + landed[k - 1]
    mine = fis.at[spot, rows_of(level), :]
    fis[spot, rows_of(level), :] = total
    ag_copies = [
        send(mine, mine, ag_send.at[k - 1], ag_recv.at[k - 1], level_peer(k))
        for k in range(1, levels)
    ]

    q_gather.relay()
    q_gather.finish()

    @pl.loop(0, low)
    def _(j):
        expand(
            lambda t: qf[tokens + t, pl.ds(j, 1), :],
            lambda t: qf[t],
            query, pl.multiple_of(j * low, low),
        )

    for copy in ag_copies:
        copy.wait_recv()
    f_gather = Gather(fis, fis_send, fis_recv)
    f_gather.relay()
    f_gather.finish()

    for i in range(GROUP):
        for k in range(BANDS):
            j = (i + k) % GROUP
            tile = fis[i, :, k * block:(k + 1) * block]
            high, rest = split(tile)
            f_high[i * block:(i + 1) * block, j * block:(j + 1) * block] = high
            f_low[i * block:(i + 1) * block, j * block:(j + 1) * block] = rest
            if 0 < k < BANDS - 1:
                high, rest = split(tile.T)
                f_high[j * block:(j + 1) * block, i * block:(i + 1) * block] = high
                f_low[j * block:(j + 1) * block, i * block:(i + 1) * block] = rest

    columns = query.shape[1]
    residual = query[...]
    direction = residual
    norm_now = jnp.sum(residual * residual, axis=0, keepdims=True)
    for sweep in range(ITERS):
        d_high, d_low = split(direction)
        both = jnp.dot(
            f_high[...], jnp.concatenate([d_high, d_low], axis=1), preferred_element_type=F32
        )
        image = (
            (jnp.dot(f_low[...], d_high, preferred_element_type=F32) + both[:, columns:])
            + both[:, :columns]
        ) + DAMPING * direction
        step_size = norm_now / jnp.sum(direction * image, axis=0, keepdims=True)
        if sweep == 0:
            x_ref[...] = step_size * direction
        else:
            x_ref[...] += step_size * direction
        if sweep + 1 < ITERS:
            residual = residual - step_size * image
            norm_next = jnp.sum(residual * residual, axis=0, keepdims=True)
            direction = residual + norm_next / norm_now * direction
            norm_now = norm_next

    own_rows = feat // count
    own_ref[...] = x_ref[pl.ds(pl.multiple_of(me * own_rows, own_rows), own_rows), :]
    x_high, x_low = split(x_ref[...])
    l_high, l_low = split(local[...])
    raw = (
        jnp.dot(l_low, x_high, preferred_element_type=F32)
        + jnp.dot(l_high, x_low, preferred_element_type=F32)
    ) + jnp.dot(l_high, x_high, preferred_element_type=F32)
    scores_ref[...] = raw * weight_ref[...] * feat ** (-0.5)

    for copy in q_copies + rs_copies + ag_copies:
        copy.wait_send()


def body(
    activations, out_grads, input_proj, output_proj, time_weight, time_index, pair_ids, query_ids
):
    pairs, tokens, width_in = activations.shape
    width_out = out_grads.shape[2]
    low = input_proj.shape[1]
    feat = low * low
    count = lax.axis_size("dp")
    levels = count // GROUP
    block = feat // GROUP
    piece = block // levels
    columns = query_ids.shape[0]
    width = 2 * tokens * low
    act_low = jnp.dot(
        activations.reshape(-1, width_in), input_proj, preferred_element_type=F32
    ).reshape(pairs, tokens * low)
    grad_low = jnp.dot(
        out_grads.reshape(-1, width_out), output_proj, preferred_element_type=F32
    ).reshape(pairs, tokens * low)
    grid = jnp.arange(time_weight.shape[0], dtype=jnp.int32)
    loss_weight = jnp.sum(
        jnp.where(time_index[:, None] == grid[None, :], time_weight[None, :], 0.0), axis=1
    )
    extras = jnp.stack([loss_weight / (pairs * count), pair_ids.astype(F32)])
    extras = jnp.pad(extras, ((0, 6), (0, width - pairs)))
    msg = jnp.concatenate([jnp.concatenate([act_low, grad_low], axis=1), extras], axis=0)
    group_pairs = GROUP * pairs
    dma = pltpu.SemaphoreType.DMA
    scratch = [
        pltpu.VMEM((GROUP, pairs + 8, width), F32),
        pltpu.VMEM((width, group_pairs), F32),
        pltpu.VMEM((width, pairs), F32),
        pltpu.VMEM((feat, pairs), F32),
        pltpu.VMEM((pairs, feat), F32),
        pltpu.VMEM((BANDS * block, group_pairs), F32),
        pltpu.VMEM((block, BANDS * block), F32),
        pltpu.VMEM((levels - 1, piece, BANDS * block), F32),
        pltpu.VMEM((GROUP, block, BANDS * block), F32),
        pltpu.VMEM((width // GROUP, columns), F32),
        pltpu.VMEM((levels - 1, width // GROUP, columns), F32),
        pltpu.VMEM((GROUP, width // GROUP, columns), F32),
        pltpu.VMEM((feat, columns), F32),
        pltpu.VMEM((feat, feat), BF16),
        pltpu.VMEM((feat, feat), BF16),
        pltpu.VMEM((feat, columns), F32),
        dma((GROUP - 1,)), dma((GROUP - 1,)),
        dma((levels - 1,)), dma((levels - 1,)),
        dma((levels - 1,)), dma((levels - 1,)),
        dma((levels - 1,)), dma((levels - 1,)),
        dma((GROUP - 1,)), dma((GROUP - 1,)),
        dma((GROUP - 1,)), dma((GROUP - 1,)),
    ]
    vmem = pl.BlockSpec(memory_space=pltpu.VMEM)
    scores, own = pl.pallas_call(
        functools.partial(kernel, count, tokens, low, pairs),
        out_shape=(
            jax.ShapeDtypeStruct((pairs, columns), F32),
            jax.ShapeDtypeStruct((feat // count, columns), F32),
        ),
        in_specs=[vmem] * 3,
        out_specs=(vmem, vmem),
        scratch_shapes=scratch,
        compiler_params=pltpu.CompilerParams(
            collective_id=0, has_side_effects=True, vmem_limit_bytes=48 * 1024 * 1024
        ),
    )(msg, query_ids.astype(F32)[:, None], loss_weight[:, None])
    return scores, own


def solution(mesh):
    placed = (
        P(("parts", "dp"), None, None),
        P(("parts", "dp"), None, None),
        P(),
        P(),
        P(),
        P(("parts", "dp")),
        P(("parts", "dp")),
        P("parts"),
    )
    return jax.shard_map(
        body,
        mesh=mesh,
        in_specs=placed,
        out_specs=(P(("parts", "dp"), None), P("dp", "parts")),
        check_vma=False,
    )
```

```python
import functools

import jax
import jax.numpy as jnp
from jax import lax
from jax.experimental import pallas as pl
from jax.experimental.pallas import tpu as pltpu
from jax.sharding import PartitionSpec as P

ITERS = 4
DAMPING = 0.5
GROUP = 8
BANDS = GROUP // 2 + 1
F32 = jnp.float32
BF16 = jnp.bfloat16


def split(value):
    high = value.astype(BF16)
    return high, (value - high.astype(F32)).astype(BF16)


def dot_nt(a, b):
    return lax.dot_general(a, b, (((1,), (1,)), ((), ())), preferred_element_type=F32)


def flip(index, bits):
    out = index
    for bit in (1, 2, 4):
        if bits & bit:
            out = out + bit - 2 * bit * ((index // bit) % 2)
    return out


def kernel(
    count, tokens, low, pairs, msg_ref, query_ref, weight_ref, scores_ref, own_ref,
    fac, fac_t, own_t, local_t, local, feats, part, landed, fis, qpart, qlanded, qf, query,
    f_high, f_low, x_ref,
    fac_send, fac_recv, rs_send, rs_recv, qz_send, qz_recv, ag_send, ag_recv,
    fis_send, fis_recv, qf_send, qf_recv,
):
    me = lax.axis_index("dp")
    spot = me % GROUP
    base = me - spot
    level = me // GROUP
    levels = count // GROUP
    feat = low * low
    block = feat // GROUP
    piece = block // levels
    per_block = block // low

    def send(src, dst, send_sem, recv_sem, peer):
        copy = pltpu.make_async_remote_copy(
            src_ref=src, dst_ref=dst, send_sem=send_sem, recv_sem=recv_sem,
            device_id={"dp": peer}, device_id_type=pl.DeviceIdType.MESH,
        )
        copy.start()
        return copy

    def level_peer(step):
        return ((level + step) % levels) * GROUP + spot

    class Gather:
        def __init__(self, buffer, spans, send_sem, recv_sem, source=None):
            self.buffer, self.spans = buffer, spans
            self.send_sem, self.recv_sem = send_sem, recv_sem
            self.source = buffer.at[spot] if source is None else source
            self.copies = {}

        def copy(self, src, slot, bits, via, n):
            self.copies[bits, n] = send(
                src, self.buffer.at[slot, self.spans[n], :],
                self.send_sem.at[bits - 1, n], self.recv_sem.at[bits - 1, n],
                base + flip(spot, via),
            )

        def own(self, n):
            for bits in (2, 4, 1):
                self.copy(self.source.at[self.spans[n], :], spot, bits, bits, n)

        def forward(self, bits, via, n):
            slot = flip(spot, bits)
            self.copy(self.buffer.at[slot, self.spans[n], :], slot, bits ^ via, via, n)

        def hop(self, n):
            for bits in (2, 4) if n % 2 == 0 else (4, 2):
                self.copies[bits, n].wait_recv()
                if bits == (2, 4)[n % 2]:
                    self.forward(bits, 6 - bits, n)
                self.forward(bits, 1, n)

        def last(self, n):
            self.copies[6, n].wait_recv()
            self.forward(6, 1, n)

        def finish(self):
            for n in range(len(self.spans)):
                for bits in (1, 3, 5, 7):
                    self.copies[bits, n].wait_recv()
            for copy in self.copies.values():
                copy.wait_send()

    barrier = pltpu.get_barrier_semaphore()
    peers = [base + flip(spot, bits) for bits in (1, 2, 4)]
    peers += [level_peer(step) for step in range(1, levels)]
    for peer in peers:
        pl.semaphore_signal(
            barrier, inc=1, device_id={"dp": peer}, device_id_type=pl.DeviceIdType.MESH
        )
    pl.semaphore_wait(barrier, len(peers))

    cut = (pairs // 16) * 8
    gather = Gather(
        fac, (pl.ds(0, cut), pl.ds(cut, pairs + 8 - cut)), fac_send, fac_recv, msg_ref
    )
    gather.own(0)
    gather.own(1)
    fac[spot] = msg_ref[...]
    gather.hop(0)
    gather.hop(1)
    gather.last(0)
    gather.last(1)
    gather.finish()

    def expand(read_row, act, out, start):
        total = None
        for t in range(tokens):
            term = read_row(t) * act(t)
            total = term if total is None else total + term
        out[pl.ds(start, low), :] = total

    half = tokens * low

    fac_t[...] = jnp.concatenate([fac[s, 0:pairs, :] for s in range(GROUP)], axis=0).T
    extras = jnp.concatenate([fac[s, pairs:pairs + 8, 0:pairs] for s in range(GROUP)], axis=1)
    weights = extras[0:1, :]
    ids = extras[1:2, :]

    chosen = jnp.where(query_ref[...] == ids, 1.0, 0.0).astype(BF16)
    share = 2 * half // GROUP
    rows = fac_t[pl.ds(pl.multiple_of(spot * share, share), share), :]
    high, rest = rows.astype(BF16), rows
    rest = rest - high.astype(F32)
    mid, last = split(rest)
    qpart[...] = (dot_nt(last, chosen) + dot_nt(mid, chosen)) + dot_nt(high, chosen)
    q_copies = [
        send(qpart, qlanded.at[k - 1], qz_send.at[k - 1], qz_recv.at[k - 1], level_peer(k))
        for k in range(1, levels)
    ]

    for b in range(BANDS):
        first = ((spot + b) % GROUP) * per_block

        @pl.loop(0, per_block)
        def _(jj):
            expand(
                lambda t: fac_t[pl.ds(half + t * low + first + jj, 1), :],
                lambda t: fac_t[t * low:(t + 1) * low, :],
                feats, pl.multiple_of(b * block + jj * low, low),
            )

    a_high, a_low = split(feats[0:block, :] * weights)
    for b in range(BANDS):
        b_high, b_low = split(feats[b * block:(b + 1) * block, :])
        part[:, b * block:(b + 1) * block] = (
            dot_nt(a_low, b_high) + dot_nt(a_high, b_low)
        ) + dot_nt(a_high, b_high)

    def rows_of(lv):
        return pl.ds(pl.multiple_of(lv * piece, piece), piece)

    rs_copies = [
        send(
            part.at[rows_of((level + k) % levels), :], landed.at[k - 1],
            rs_send.at[k - 1], rs_recv.at[k - 1], level_peer(k),
        )
        for k in range(1, levels)
    ]
    own_t[...] = msg_ref[0:pairs, :].T

    @pl.loop(0, low)
    def _(j):
        expand(
            lambda t: own_t[pl.ds(half + t * low + j, 1), :],
            lambda t: own_t[t * low:(t + 1) * low, :],
            local_t, pl.multiple_of(j * low, low),
        )

    local[...] = local_t[...].T

    q_total = qpart[...]
    for k in range(1, levels):
        q_copies[k - 1].wait_recv()
        q_total = q_total + qlanded[k - 1]
    qf[spot] = q_total
    q_gather = Gather(qf, (pl.ds(0, share),), qf_send, qf_recv)
    q_gather.own(0)

    total = part[rows_of(level), :]
    for k in range(1, levels):
        rs_copies[k - 1].wait_recv()
        total = total + landed[k - 1]
    mine = fis.at[spot, rows_of(level), :]
    fis[spot, rows_of(level), :] = total
    ag_copies = [
        send(mine, mine, ag_send.at[k - 1], ag_recv.at[k - 1], level_peer(k))
        for k in range(1, levels)
    ]

    f_gather = Gather(
        fis, [rows_of((level + n) % levels) for n in range(levels)], fis_send, fis_recv
    )
    f_gather.own(0)
    q_gather.hop(0)
    for n in range(1, levels):
        ag_copies[levels - n - 1].wait_recv()
        f_gather.own(n)
        f_gather.hop(n - 1)
        if n >= 2:
            f_gather.last(n - 2)
    f_gather.hop(levels - 1)
    if levels > 1:
        f_gather.last(levels - 2)
    f_gather.last(levels - 1)
    q_gather.last(0)
    q_gather.finish()

    @pl.loop(0, low)
    def _(j):
        expand(
            lambda t: qf[tokens + t, pl.ds(j, 1), :],
            lambda t: qf[t],
            query, pl.multiple_of(j * low, low),
        )

    f_gather.finish()

    for i in range(GROUP):
        for k in range(BANDS):
            j = (i + k) % GROUP
            tile = fis[i, :, k * block:(k + 1) * block]
            high, rest = split(tile)
            f_high[i * block:(i + 1) * block, j * block:(j + 1) * block] = high
            f_low[i * block:(i + 1) * block, j * block:(j + 1) * block] = rest
            if 0 < k < BANDS - 1:
                high, rest = split(tile.T)
                f_high[j * block:(j + 1) * block, i * block:(i + 1) * block] = high
                f_low[j * block:(j + 1) * block, i * block:(i + 1) * block] = rest

    columns = query.shape[1]
    residual = query[...]
    direction = residual
    norm_now = jnp.sum(residual * residual, axis=0, keepdims=True)
    for sweep in range(ITERS):
        d_high, d_low = split(direction)
        both = jnp.dot(
            f_high[...], jnp.concatenate([d_high, d_low], axis=1), preferred_element_type=F32
        )
        image = (
            (jnp.dot(f_low[...], d_high, preferred_element_type=F32) + both[:, columns:])
            + both[:, :columns]
        ) + DAMPING * direction
        step_size = norm_now / jnp.sum(direction * image, axis=0, keepdims=True)
        if sweep == 0:
            x_ref[...] = step_size * direction
        else:
            x_ref[...] += step_size * direction
        if sweep + 1 < ITERS:
            residual = residual - step_size * image
            norm_next = jnp.sum(residual * residual, axis=0, keepdims=True)
            direction = residual + norm_next / norm_now * direction
            norm_now = norm_next

    own_rows = feat // count
    own_ref[...] = x_ref[pl.ds(pl.multiple_of(me * own_rows, own_rows), own_rows), :]
    x_high, x_low = split(x_ref[...])
    l_high, l_low = split(local[...])
    raw = (
        jnp.dot(l_low, x_high, preferred_element_type=F32)
        + jnp.dot(l_high, x_low, preferred_element_type=F32)
    ) + jnp.dot(l_high, x_high, preferred_element_type=F32)
    scores_ref[...] = raw * weight_ref[...] * feat ** (-0.5)

    for copy in q_copies + rs_copies + ag_copies:
        copy.wait_send()


def body(
    activations, out_grads, input_proj, output_proj, time_weight, time_index, pair_ids, query_ids
):
    pairs, tokens, width_in = activations.shape
    width_out = out_grads.shape[2]
    low = input_proj.shape[1]
    feat = low * low
    count = lax.axis_size("dp")
    levels = count // GROUP
    block = feat // GROUP
    piece = block // levels
    columns = query_ids.shape[0]
    width = 2 * tokens * low
    act_low = jnp.einsum(
        "ptk,ki->pti", activations, input_proj, preferred_element_type=F32
    )
    grad_low = jnp.einsum(
        "ptk,ki->pti", out_grads, output_proj, preferred_element_type=F32
    )
    act_low, grad_low = lax.optimization_barrier((act_low, grad_low))
    act_low = act_low.reshape(pairs, tokens * low)
    grad_low = grad_low.reshape(pairs, tokens * low)
    grid = jnp.arange(time_weight.shape[0], dtype=jnp.int32)
    loss_weight = jnp.sum(
        jnp.where(time_index[:, None] == grid[None, :], time_weight[None, :], 0.0), axis=1
    )
    extras = jnp.stack([loss_weight / (pairs * count), pair_ids.astype(F32)])
    extras = jnp.pad(extras, ((0, 6), (0, width - pairs)))
    msg = jnp.concatenate([jnp.concatenate([act_low, grad_low], axis=1), extras], axis=0)
    group_pairs = GROUP * pairs
    dma = pltpu.SemaphoreType.DMA
    scratch = [
        pltpu.VMEM((GROUP, pairs + 8, width), F32),
        pltpu.VMEM((width, group_pairs), F32),
        pltpu.VMEM((width, pairs), F32),
        pltpu.VMEM((feat, pairs), F32),
        pltpu.VMEM((pairs, feat), F32),
        pltpu.VMEM((BANDS * block, group_pairs), F32),
        pltpu.VMEM((block, BANDS * block), F32),
        pltpu.VMEM((levels - 1, piece, BANDS * block), F32),
        pltpu.VMEM((GROUP, block, BANDS * block), F32),
        pltpu.VMEM((width // GROUP, columns), F32),
        pltpu.VMEM((levels - 1, width // GROUP, columns), F32),
        pltpu.VMEM((GROUP, width // GROUP, columns), F32),
        pltpu.VMEM((feat, columns), F32),
        pltpu.VMEM((feat, feat), BF16),
        pltpu.VMEM((feat, feat), BF16),
        pltpu.VMEM((feat, columns), F32),
        dma((GROUP - 1, 2)), dma((GROUP - 1, 2)),
        dma((levels - 1,)), dma((levels - 1,)),
        dma((levels - 1,)), dma((levels - 1,)),
        dma((levels - 1,)), dma((levels - 1,)),
        dma((GROUP - 1, levels)), dma((GROUP - 1, levels)),
        dma((GROUP - 1, 1)), dma((GROUP - 1, 1)),
    ]
    vmem = pl.BlockSpec(memory_space=pltpu.VMEM)
    scores, own = pl.pallas_call(
        functools.partial(kernel, count, tokens, low, pairs),
        out_shape=(
            jax.ShapeDtypeStruct((pairs, columns), F32),
            jax.ShapeDtypeStruct((feat // count, columns), F32),
        ),
        in_specs=[vmem] * 3,
        out_specs=(vmem, vmem),
        scratch_shapes=scratch,
        compiler_params=pltpu.CompilerParams(
            collective_id=0, has_side_effects=True, vmem_limit_bytes=48 * 1024 * 1024
        ),
    )(msg, query_ids.astype(F32)[:, None], loss_weight[:, None])
    return scores, own


def solution(mesh):
    placed = (
        P(("parts", "dp"), None, None),
        P(("parts", "dp"), None, None),
        P(),
        P(),
        P(),
        P(("parts", "dp")),
        P(("parts", "dp")),
        P("parts"),
    )
    return jax.shard_map(
        body,
        mesh=mesh,
        in_specs=placed,
        out_specs=(P(("parts", "dp"), None), P("dp", "parts")),
        check_vma=False,
    )
```

```python
import functools

import jax
import jax.numpy as jnp
from jax import lax
from jax.experimental import pallas as pl
from jax.experimental.pallas import tpu as pltpu
from jax.sharding import PartitionSpec as P

ITERS = 4
DAMPING = 0.5
GROUP = 8
BANDS = GROUP // 2 + 1
F32 = jnp.float32
BF16 = jnp.bfloat16


def split(value):
    high = value.astype(BF16)
    return high, (value - high.astype(F32)).astype(BF16)


def dot_nt(a, b):
    return lax.dot_general(a, b, (((1,), (1,)), ((), ())), preferred_element_type=F32)


def flip(index, bits):
    out = index
    for bit in (1, 2, 4):
        if bits & bit:
            out = out + bit - 2 * bit * ((index // bit) % 2)
    return out


def kernel(
    count, tokens, low, pairs, msg_ref, query_ref, weight_ref, scores_ref, own_ref,
    fac, fac_t, own_t, local_t, local, feats, part, landed, fis, qpart, qlanded, qf, query,
    f_high, f_low, x_ref,
    fac_send, fac_recv, rs_send, rs_recv, qz_send, qz_recv, ag_send, ag_recv,
    fis_send, fis_recv, qf_send, qf_recv,
):
    me = lax.axis_index("dp")
    spot = me % GROUP
    base = me - spot
    level = me // GROUP
    levels = count // GROUP
    feat = low * low
    block = feat // GROUP
    piece = block // levels
    per_block = block // low

    def send(src, dst, send_sem, recv_sem, peer):
        copy = pltpu.make_async_remote_copy(
            src_ref=src, dst_ref=dst, send_sem=send_sem, recv_sem=recv_sem,
            device_id={"dp": peer}, device_id_type=pl.DeviceIdType.MESH,
        )
        copy.start()
        return copy

    def level_peer(step):
        return ((level + step) % levels) * GROUP + spot

    class Gather:
        def __init__(self, buffer, spans, send_sem, recv_sem, source=None):
            self.buffer, self.spans = buffer, spans
            self.send_sem, self.recv_sem = send_sem, recv_sem
            self.source = buffer.at[spot] if source is None else source
            self.copies = {}

        def copy(self, src, slot, bits, via, n):
            self.copies[bits, n] = send(
                src, self.buffer.at[slot, self.spans[n], :],
                self.send_sem.at[bits - 1, n], self.recv_sem.at[bits - 1, n],
                base + flip(spot, via),
            )

        def own(self, n):
            for bits in (2, 4, 1):
                self.copy(self.source.at[self.spans[n], :], spot, bits, bits, n)

        def forward(self, bits, via, n):
            slot = flip(spot, bits)
            self.copy(self.buffer.at[slot, self.spans[n], :], slot, bits ^ via, via, n)

        def hop(self, n):
            for bits in (2, 4) if n % 2 == 0 else (4, 2):
                self.copies[bits, n].wait_recv()
                if bits == (2, 4)[n % 2]:
                    self.forward(bits, 6 - bits, n)
                self.forward(bits, 1, n)

        def last(self, n):
            self.copies[6, n].wait_recv()
            self.forward(6, 1, n)

        def finish(self):
            for n in range(len(self.spans)):
                for bits in (1, 3, 5, 7):
                    self.copies[bits, n].wait_recv()
            for copy in self.copies.values():
                copy.wait_send()

    barrier = pltpu.get_barrier_semaphore()
    peers = [base + flip(spot, bits) for bits in (1, 2, 4)]
    peers += [level_peer(step) for step in range(1, levels)]
    for peer in peers:
        pl.semaphore_signal(
            barrier, inc=1, device_id={"dp": peer}, device_id_type=pl.DeviceIdType.MESH
        )
    pl.semaphore_wait(barrier, len(peers))

    cut = (pairs // 16) * 8
    gather = Gather(
        fac, (pl.ds(0, cut), pl.ds(cut, pairs + 8 - cut)), fac_send, fac_recv, msg_ref
    )
    gather.own(0)
    gather.own(1)
    fac[spot] = msg_ref[...]
    gather.hop(0)
    gather.hop(1)
    gather.last(0)
    gather.last(1)
    gather.finish()

    def expand(read_row, act, out, start):
        total = None
        for t in range(tokens):
            term = read_row(t) * act(t)
            total = term if total is None else total + term
        out[pl.ds(start, low), :] = total

    half = tokens * low

    fac_t[...] = jnp.concatenate([fac[s, 0:pairs, :] for s in range(GROUP)], axis=0).T
    extras = jnp.concatenate([fac[s, pairs:pairs + 8, 0:pairs] for s in range(GROUP)], axis=1)
    weights = extras[0:1, :]
    ids = extras[1:2, :]

    chosen = jnp.where(query_ref[...] == ids, 1.0, 0.0).astype(BF16)
    share = 2 * half // GROUP
    rows = fac_t[pl.ds(pl.multiple_of(spot * share, share), share), :]
    high, rest = rows.astype(BF16), rows
    rest = rest - high.astype(F32)
    mid, last = split(rest)
    qpart[...] = (dot_nt(last, chosen) + dot_nt(mid, chosen)) + dot_nt(high, chosen)
    q_copies = [
        send(qpart, qlanded.at[k - 1], qz_send.at[k - 1], qz_recv.at[k - 1], level_peer(k))
        for k in range(1, levels)
    ]

    def rows_of(lv):
        return pl.ds(pl.multiple_of(lv * piece, piece), piece)

    rs_copies = []
    for b in range(BANDS):
        first = ((spot + b) % GROUP) * per_block
        band = pl.ds(b * block, block)

        @pl.loop(0, per_block)
        def _(jj):
            expand(
                lambda t: fac_t[pl.ds(half + t * low + first + jj, 1), :],
                lambda t: fac_t[t * low:(t + 1) * low, :],
                feats, pl.multiple_of(b * block + jj * low, low),
            )

        if b == 0:
            a_high, a_low = split(feats[0:block, :] * weights)
        b_high, b_low = split(feats[b * block:(b + 1) * block, :])
        part[:, b * block:(b + 1) * block] = (
            dot_nt(a_low, b_high) + dot_nt(a_high, b_low)
        ) + dot_nt(a_high, b_high)
        rs_copies += [
            send(
                part.at[rows_of((level + k) % levels), band], landed.at[k - 1, :, band],
                rs_send.at[b, k - 1], rs_recv.at[b, k - 1], level_peer(k),
            )
            for k in range(1, levels)
        ]

    own_t[...] = msg_ref[0:pairs, :].T

    @pl.loop(0, low)
    def _(j):
        expand(
            lambda t: own_t[pl.ds(half + t * low + j, 1), :],
            lambda t: own_t[t * low:(t + 1) * low, :],
            local_t, pl.multiple_of(j * low, low),
        )

    local[...] = local_t[...].T

    q_total = qpart[...]
    for k in range(1, levels):
        q_copies[k - 1].wait_recv()
        q_total = q_total + qlanded[k - 1]
    qf[spot] = q_total
    q_gather = Gather(qf, (pl.ds(0, share),), qf_send, qf_recv)
    q_gather.own(0)

    for copy in rs_copies:
        copy.wait_recv()
    total = part[rows_of(level), :]
    for k in range(1, levels):
        total = total + landed[k - 1]
    mine = fis.at[spot, rows_of(level), :]
    fis[spot, rows_of(level), :] = total
    ag_copies = [
        send(mine, mine, ag_send.at[k - 1], ag_recv.at[k - 1], level_peer(k))
        for k in range(1, levels)
    ]

    f_gather = Gather(
        fis, [rows_of((level + n) % levels) for n in range(levels)], fis_send, fis_recv
    )
    f_gather.own(0)
    q_gather.hop(0)
    for n in range(1, levels):
        ag_copies[levels - n - 1].wait_recv()
        f_gather.own(n)
        f_gather.hop(n - 1)
        if n >= 2:
            f_gather.last(n - 2)
    f_gather.hop(levels - 1)
    if levels > 1:
        f_gather.last(levels - 2)
    f_gather.last(levels - 1)
    q_gather.last(0)
    q_gather.finish()

    @pl.loop(0, low)
    def _(j):
        expand(
            lambda t: qf[tokens + t, pl.ds(j, 1), :],
            lambda t: qf[t],
            query, pl.multiple_of(j * low, low),
        )

    f_gather.finish()

    for i in range(GROUP):
        for k in range(BANDS):
            j = (i + k) % GROUP
            tile = fis[i, :, k * block:(k + 1) * block]
            high, rest = split(tile)
            f_high[i * block:(i + 1) * block, j * block:(j + 1) * block] = high
            f_low[i * block:(i + 1) * block, j * block:(j + 1) * block] = rest
            if 0 < k < BANDS - 1:
                high, rest = split(tile.T)
                f_high[j * block:(j + 1) * block, i * block:(i + 1) * block] = high
                f_low[j * block:(j + 1) * block, i * block:(i + 1) * block] = rest

    columns = query.shape[1]
    residual = query[...]
    direction = residual
    norm_now = jnp.sum(residual * residual, axis=0, keepdims=True)
    for sweep in range(ITERS):
        d_high, d_low = split(direction)
        both = jnp.dot(
            f_high[...], jnp.concatenate([d_high, d_low], axis=1), preferred_element_type=F32
        )
        image = (
            (jnp.dot(f_low[...], d_high, preferred_element_type=F32) + both[:, columns:])
            + both[:, :columns]
        ) + DAMPING * direction
        step_size = norm_now / jnp.sum(direction * image, axis=0, keepdims=True)
        if sweep == 0:
            x_ref[...] = step_size * direction
        else:
            x_ref[...] += step_size * direction
        if sweep + 1 < ITERS:
            residual = residual - step_size * image
            norm_next = jnp.sum(residual * residual, axis=0, keepdims=True)
            direction = residual + norm_next / norm_now * direction
            norm_now = norm_next

    own_rows = feat // count
    own_ref[...] = x_ref[pl.ds(pl.multiple_of(me * own_rows, own_rows), own_rows), :]
    x_high, x_low = split(x_ref[...])
    l_high, l_low = split(local[...])
    raw = (
        jnp.dot(l_low, x_high, preferred_element_type=F32)
        + jnp.dot(l_high, x_low, preferred_element_type=F32)
    ) + jnp.dot(l_high, x_high, preferred_element_type=F32)
    scores_ref[...] = raw * weight_ref[...] * feat ** (-0.5)

    for copy in q_copies + rs_copies + ag_copies:
        copy.wait_send()


def body(
    activations, out_grads, input_proj, output_proj, time_weight, time_index, pair_ids, query_ids
):
    pairs, tokens, width_in = activations.shape
    width_out = out_grads.shape[2]
    low = input_proj.shape[1]
    feat = low * low
    count = lax.axis_size("dp")
    levels = count // GROUP
    block = feat // GROUP
    piece = block // levels
    columns = query_ids.shape[0]
    width = 2 * tokens * low
    act_low = jnp.einsum(
        "ptk,ki->pti", activations, input_proj, preferred_element_type=F32
    )
    grad_low = jnp.einsum(
        "ptk,ki->pti", out_grads, output_proj, preferred_element_type=F32
    )
    act_low, grad_low = lax.optimization_barrier((act_low, grad_low))
    act_low = act_low.reshape(pairs, tokens * low)
    grad_low = grad_low.reshape(pairs, tokens * low)
    grid = jnp.arange(time_weight.shape[0], dtype=jnp.int32)
    loss_weight = jnp.sum(
        jnp.where(time_index[:, None] == grid[None, :], time_weight[None, :], 0.0), axis=1
    )
    extras = jnp.stack([loss_weight / (pairs * count), pair_ids.astype(F32)])
    extras = jnp.pad(extras, ((0, 6), (0, width - pairs)))
    msg = jnp.concatenate([jnp.concatenate([act_low, grad_low], axis=1), extras], axis=0)
    group_pairs = GROUP * pairs
    dma = pltpu.SemaphoreType.DMA
    scratch = [
        pltpu.VMEM((GROUP, pairs + 8, width), F32),
        pltpu.VMEM((width, group_pairs), F32),
        pltpu.VMEM((width, pairs), F32),
        pltpu.VMEM((feat, pairs), F32),
        pltpu.VMEM((pairs, feat), F32),
        pltpu.VMEM((BANDS * block, group_pairs), F32),
        pltpu.VMEM((block, BANDS * block), F32),
        pltpu.VMEM((levels - 1, piece, BANDS * block), F32),
        pltpu.VMEM((GROUP, block, BANDS * block), F32),
        pltpu.VMEM((width // GROUP, columns), F32),
        pltpu.VMEM((levels - 1, width // GROUP, columns), F32),
        pltpu.VMEM((GROUP, width // GROUP, columns), F32),
        pltpu.VMEM((feat, columns), F32),
        pltpu.VMEM((feat, feat), BF16),
        pltpu.VMEM((feat, feat), BF16),
        pltpu.VMEM((feat, columns), F32),
        dma((GROUP - 1, 2)), dma((GROUP - 1, 2)),
        dma((BANDS, levels - 1)), dma((BANDS, levels - 1)),
        dma((levels - 1,)), dma((levels - 1,)),
        dma((levels - 1,)), dma((levels - 1,)),
        dma((GROUP - 1, levels)), dma((GROUP - 1, levels)),
        dma((GROUP - 1, 1)), dma((GROUP - 1, 1)),
    ]
    vmem = pl.BlockSpec(memory_space=pltpu.VMEM)
    scores, own = pl.pallas_call(
        functools.partial(kernel, count, tokens, low, pairs),
        out_shape=(
            jax.ShapeDtypeStruct((pairs, columns), F32),
            jax.ShapeDtypeStruct((feat // count, columns), F32),
        ),
        in_specs=[vmem] * 3,
        out_specs=(vmem, vmem),
        scratch_shapes=scratch,
        compiler_params=pltpu.CompilerParams(
            collective_id=0, has_side_effects=True, vmem_limit_bytes=48 * 1024 * 1024
        ),
    )(msg, query_ids.astype(F32)[:, None], loss_weight[:, None])
    return scores, own


def solution(mesh):
    placed = (
        P(("parts", "dp"), None, None),
        P(("parts", "dp"), None, None),
        P(),
        P(),
        P(),
        P(("parts", "dp")),
        P(("parts", "dp")),
        P("parts"),
    )
    return jax.shard_map(
        body,
        mesh=mesh,
        in_specs=placed,
        out_specs=(P(("parts", "dp"), None), P("dp", "parts")),
        check_vma=False,
    )
```
